32 devices in a mesh: grp: 2 (over y), blk: 16 (over z, x, core).
Axes of the slice: x: 2, y: 2, z: 4, core: 2. Of those that a mesh axis runs over, the one named last changes fastest.
Arguments:
- doc_grads: bfloat16 [16384, 8192], P(('grp', 'blk')), parts along dimension 0, may hold values from -6 to 6
- val_grads: bfloat16 [16, 8192], P('blk'), may hold values from -0.0625 to 0.0625
- inv_hessian: bfloat16 [8192, 8192], P('blk'), as said below
- topic_mask: int32 [128, 16], P(('grp', 'blk')), parts along dimension 0, may hold values 0 or 1
- membership: int32 [16384], P(('grp', 'blk')), parts along dimension 0, may hold values from 0 to 127
- owner_slot: int32 [128], replicated, may hold values from 0 to 127, each once
Outputs:
- cluster_influence: float32 [256, 16], P(('grp', 'blk')), parts along dimension 0
The draws below stay inside these ranges and needn't reach their ends.
There are 2 independent parts, one for each index of `grp`. The reference program is written for one: setup_inputs(seed, part) draws one part's arguments, and reference() takes and returns one part's arrays. A program takes and returns all parts, laid end to end along the dimension named above; an argument that names none is the same for every part. Nothing has to cross between parts.
Inputs may be any that keep to these rules, and one draw needn't show every extreme that they name: inv_hessian is symmetric. `owner_slot`: each output row is the slot of exactly one cluster.
All inputs are finite; a program needn't handle non-finite values. No bound on the sum of `topic_mask` on one device may be relied on, other than what follows from the above.
Results may differ from the reference program's by a relative error of at most 0.0055.
Values may be sent and summed in bfloat16 or wider, within the bound.
No kernel may reach another device: no remote copies, remote signals or barrier semaphores. Data moves between devices by JAX's collectives and lax.ppermute only.
A program may use at most 64 MiB of HBM per device.

```python
import jax
import jax.numpy as jnp
from jax import lax

P_SIZE = 8192
DOC_BLK = 128
VAL_DEV = 1
DOCS = 8192
VAL = 16
CLUSTERS = 128
DOC_BLOCKS = 64


def draw_inv_hessian(key, part):
    key = jax.random.fold_in(key, 11)
    key_diag = jax.random.fold_in(key, 1)
    key_off = jax.random.fold_in(key, 2)
    diag_vals = jax.random.uniform(key_diag, (P_SIZE,), jnp.float32, 1.5, 3.0)
    noise = jax.random.normal(key_off, (P_SIZE, P_SIZE), jnp.float32) * (0.5 / P_SIZE ** 0.5)
    symmetric = (noise + noise.T) * 0.7071
    rows = lax.broadcasted_iota(jnp.int32, (P_SIZE, P_SIZE), 0)
    columns = lax.broadcasted_iota(jnp.int32, (P_SIZE, P_SIZE), 1)
    full = jnp.where(rows == columns, diag_vals[:, None], symmetric)
    return full.astype(jnp.bfloat16)


def place_ends(result, own_key, low, largest):
    longest = result.shape.index(max(result.shape))
    spots = []
    for shift in (0, 1):
        where = [jax.random.randint(jax.random.fold_in(own_key, axis), (), 0, length) for axis, length in enumerate(result.shape)]
        where[longest] = (where[longest] + shift) % result.shape[longest]
        spots.append(tuple(where))
    return result.at[spots[0]].set(low).at[spots[1]].set(largest)


def block_levels(key, shape, pieces, smallest, high):
    def one(dim, blocks):
        heights = jax.random.uniform(jax.random.fold_in(jax.random.fold_in(key, 6), dim), (blocks,), jnp.float32, smallest / len(pieces), high / len(pieces))
        return jnp.repeat(jnp.exp(heights), shape[dim] // blocks).reshape((-1,) + (1,) * (len(shape) - dim - 1))

    factor_of = one(*pieces[0])
    for cut in pieces[1:]:
        factor_of = factor_of * one(*cut)
    return factor_of


def centred(stream_key, extent, scale, most, pieces=(), kind=jnp.bfloat16):
    factor_of = block_levels(stream_key, extent, pieces, -0.22, 0.18) if pieces else 1.0
    entries = jax.random.normal(stream_key, extent, jnp.float32) * scale * factor_of
    return jnp.minimum(jnp.maximum(entries, -most), most).astype(kind)


def setup_inputs(seed: int = 0, part: int = 0) -> dict:
    splits = jax.random.split(jax.random.key(seed), 7)
    part_splits = jax.random.split(jax.random.fold_in(splits[6], part), 7)
    doc_grads = centred(part_splits[0], (DOCS, P_SIZE), 1.0, 6.0, ((0, 16),))
    val_grads = centred(splits[1], (VAL, P_SIZE), P_SIZE ** -0.5, 0.0625, ((0, 16),))
    inv_hessian = draw_inv_hessian(jax.random.fold_in(splits[6], 71), part)
    topic_mask = place_ends((jax.random.randint(part_splits[3], (DOC_BLOCKS, VAL // VAL_DEV), 0, 2) < 1).astype(jnp.int32), jax.random.fold_in(part_splits[3], 1), 0, 1)
    membership = place_ends(jax.random.randint(part_splits[4], (DOCS,), 0, CLUSTERS), jax.random.fold_in(part_splits[4], 1), 0, CLUSTERS - 1).astype(jnp.int32)
    owner_slot = jax.random.permutation(splits[5], CLUSTERS).astype(jnp.int32)
    return dict(doc_grads=doc_grads, val_grads=val_grads, inv_hessian=inv_hessian, topic_mask=topic_mask, membership=membership, owner_slot=owner_slot)


def reference(doc_grads, val_grads, inv_hessian, topic_mask, membership, owner_slot):
    precond = jnp.dot(val_grads, inv_hessian, preferred_element_type=jnp.float32).astype(jnp.bfloat16)
    scores = lax.dot_general(doc_grads, precond, (((1,), (1,)), ((), ())), preferred_element_type=jnp.float32)
    mask_full = jnp.repeat(jnp.repeat(topic_mask.astype(jnp.float32), DOC_BLK, axis=0), VAL_DEV, axis=1)
    masked = scores * mask_full
    slots = owner_slot[membership]
    summed = jax.ops.segment_sum(masked, slots, num_segments=CLUSTERS)
    return 0.125 * summed
```

```python
import jax
import jax.numpy as jnp
from jax import lax
from jax.sharding import PartitionSpec as P


def send(x, size, mask):
    return lax.ppermute(x, "blk", [(i, i ^ mask) for i in range(size)])


def split(size):
    inner = 1
    while inner * inner * 4 <= size:
        inner *= 2
    return size // inner, inner


def per_device(doc_grads, val_grads, inv_hessian, topic_mask, membership, owner_slot, *, size):
    outer, inner = split(size)
    me = lax.axis_index("blk")
    docs = doc_grads.shape[0]
    val_local, width = val_grads.shape
    rows = inv_hessian.shape[0]
    clusters = owner_slot.shape[0]
    kept = clusters // size
    order = me ^ jnp.arange(size)

    def gather(x):
        far = jnp.stack([x] + [send(x, size, s * inner) for s in range(1, outer)])
        near = jnp.stack([far] + [send(far, size, t) for t in range(1, inner)], axis=1)
        return near.reshape((size,) + x.shape)

    vals = gather(val_grads)
    vals = vals.reshape(size * val_local, width)
    panel = lax.dot_general(
        vals, inv_hessian, (((1,), (1,)), ((), ())), preferred_element_type=jnp.float32
    ).astype(jnp.bfloat16)
    panel = panel.reshape(size, val_local, rows)[order].reshape(size * val_local, rows)
    panels = gather(panel)[order]
    precond = jnp.moveaxis(panels, 0, 1).reshape(size * val_local, width)
    scores = lax.dot_general(
        precond, doc_grads, (((1,), (1,)), ((), ())), preferred_element_type=jnp.float32
    )
    block_rows = docs // topic_mask.shape[0]
    mask = jnp.repeat(topic_mask.T.astype(jnp.float32), block_rows, axis=1)
    mask = jnp.repeat(mask, val_local, axis=0)
    masked = scores * mask
    slot_of = (order[:, None] * kept + jnp.arange(kept)[None, :]).reshape(-1)
    by_slot = (slot_of[:, None] == owner_slot[None, :]).astype(jnp.bfloat16)
    by_doc = (jnp.arange(clusters)[:, None] == membership[None, :]).astype(jnp.bfloat16)
    one_hot = jnp.dot(by_slot, by_doc, preferred_element_type=jnp.float32).astype(jnp.bfloat16)
    high = masked.astype(jnp.bfloat16)
    low = (masked - high.astype(jnp.float32)).astype(jnp.bfloat16)
    dims = (((1,), (1,)), ((), ()))
    sums = lax.dot_general(one_hot, high, dims, preferred_element_type=jnp.float32)
    sums = sums + lax.dot_general(one_hot, low, dims, preferred_element_type=jnp.float32)
    sums = 0.125 * sums
    sums = sums.reshape(outer, inner * kept, -1)
    near = sums[0]
    for s in range(1, outer):
        near = near + send(sums[s], size, s * inner)
    near = near.reshape(inner, kept, -1)
    total = near[0]
    for t in range(1, inner):
        total = total + send(near[t], size, t)
    return total


def solution(mesh):
    size = mesh.shape["blk"]

    def run(*args):
        return per_device(*args, size=size)

    in_specs = (
        P(("grp", "blk"), None),
        P("blk", None),
        P("blk", None),
        P(("grp", "blk"), None),
        P(("grp", "blk")),
        P(),
    )
    out_specs = P(("grp", "blk"), None)
    return jax.shard_map(run, mesh=mesh, in_specs=in_specs, out_specs=out_specs, check_vma=False)
```

```python
import functools

import jax
import jax.numpy as jnp
from jax import lax
from jax.experimental import pallas as pl
from jax.experimental.pallas import tpu as pltpu
from jax.sharding import PartitionSpec as P

ROWS_BY_ROWS = (((1,), (1,)), ((), ()))
VMEM = pl.BlockSpec(memory_space=pltpu.VMEM)
HBM = pl.BlockSpec(memory_space=pltpu.HBM)
SMEM = pl.BlockSpec(memory_space=pltpu.SMEM)


def dot(a, b, dims=ROWS_BY_ROWS):
    return lax.dot_general(a, b, dims, preferred_element_type=jnp.float32)


def near_memory(x):
    return pltpu.with_memory_space_constraint(x, pltpu.VMEM)


def far_memory(x):
    return pltpu.with_memory_space_constraint(x, pltpu.HBM)


def call(body, name, out_shape, flops, moved, limit=12):
    return functools.partial(
        pl.pallas_call,
        body,
        out_shape=out_shape,
        compiler_params=pltpu.CompilerParams(vmem_limit_bytes=limit << 20),
        cost_estimate=pl.CostEstimate(flops=flops, bytes_accessed=moved, transcendentals=0),
        name=name,
    )


def send(x, size, mask):
    return lax.ppermute(x, "blk", [(i, i ^ mask) for i in range(size)])


def start_copies(ref, start, out, sems):
    pieces = sems.shape[0]
    rows = out.shape[0] // pieces
    copies = []
    for i in range(pieces):
        here, there = pl.ds(start + i * rows, rows), pl.ds(i * rows, rows)
        copies.append(pltpu.make_async_copy(ref.at[here], out.at[there], sems.at[i]))
        copies[-1].start()
    return copies


def fetch(x, after):
    def body(x_ref, _, out_ref, sems):
        for copy in start_copies(x_ref, 0, out_ref, sems):
            copy.wait()

    run = call(body, "fetch", pltpu.VMEM(x.shape, x.dtype), 0, 2 * x.size * x.dtype.itemsize, 1)(
        in_specs=[HBM, pl.BlockSpec(memory_space=pl.ANY)], out_specs=VMEM, scratch_shapes=[pltpu.SemaphoreType.DMA((1,))]
    )
    return near_memory(run(far_memory(x), after))


def split(size):
    inner = 1
    while inner * inner * 4 <= size:
        inner *= 2
    return size // inner, inner


def far_masks(size):
    outer, inner = split(size)
    return [s * inner + (s > 0 and inner > 1) for s in range(outer)]


def pack_body(*refs):
    out = refs[-1]
    out[...] = jnp.concatenate([r[...].astype(jnp.float32) for r in refs[:-1]], axis=0).astype(out.dtype)


def panel_body(me_ref, *refs, outer, inner):
    parts, hess_ref, docs_ref = refs[:inner], refs[inner], refs[inner + 1]
    out_ref, docs_out, sems = refs[inner + 2 :]
    copies = start_copies(docs_ref, 0, docs_out, sems)
    vals = jnp.concatenate([r[...].astype(jnp.float32) for r in parts], axis=0).astype(jnp.bfloat16)
    count = vals.shape[0]
    each = count // (outer * inner)
    to = lax.broadcasted_iota(jnp.int32, (count, count), 0)
    at = lax.broadcasted_iota(jnp.int32, (count, count), 1)
    block = at // each
    s = block % outer
    origin = me_ref[0] ^ (s * inner + jnp.where(s > 0, int(inner > 1), 0)) ^ (block // outer)
    place = (to == origin * each + at % each).astype(jnp.float32).astype(jnp.bfloat16)
    out_ref[...] = dot(place, dot(hess_ref[...], vals).astype(jnp.bfloat16)).astype(out_ref.dtype)
    for copy in copies:
        copy.wait()


def scores_of(me, docs_ref, slices_ref, step, inner):
    outer, _, rows = slices_ref.shape
    total = None
    for s, mask in enumerate(far_masks(outer * inner)):
        column = pl.multiple_of((me ^ mask ^ step) * rows, rows)
        part = dot(slices_ref[s], docs_ref[:, pl.ds(column, rows)])
        total = part if total is None else total + part
    return total


def add_scores(me, docs_refs, slices_ref, step, inner):
    return jnp.concatenate([scores_of(me, r, slices_ref, step, inner) for r in docs_refs], axis=1)


def first_body(
    me_ref, low_ref, docs_ref, slices_ref, mask_ref, member_ref, slot_ref, out_ref, hot_ref, wide_ref, high_ref, sems, *, inner
):
    split_at = low_ref.shape[0]
    copies = start_copies(docs_ref, split_at, high_ref, sems)
    out_ref[:, :split_at] = scores_of(me_ref[0], low_ref, slices_ref, 0, inner)
    clusters, docs = hot_ref.shape
    row = lax.broadcasted_iota(jnp.int32, (clusters, clusters), 0)
    by_slot = (row == slot_ref[...]).astype(jnp.float32).astype(jnp.bfloat16)
    cluster = lax.broadcasted_iota(jnp.int32, (clusters, docs), 0)
    by_doc = (cluster == member_ref[...]).astype(jnp.float32).astype(jnp.bfloat16)
    hot_ref[...] = dot(by_slot, by_doc, (((1,), (0,)), ((), ()))).astype(jnp.bfloat16)
    blocks = mask_ref.shape[0]
    doc = lax.broadcasted_iota(jnp.int32, (blocks, docs), 1)
    spread = (doc // (docs // blocks) == lax.broadcasted_iota(jnp.int32, (blocks, docs), 0)).astype(jnp.float32)
    narrow = mask_ref[...].astype(jnp.float32)
    wide_ref[...] = dot(narrow.astype(jnp.bfloat16), spread.astype(jnp.bfloat16), (((0,), (0,)), ((), ())))
    for copy in copies:
        copy.wait()
    out_ref[:, split_at:] = scores_of(me_ref[0], high_ref, slices_ref, 0, inner)


def next_body(me_ref, low_ref, high_ref, slices_ref, sum_ref, out_ref, *, step, inner):
    out_ref[...] = sum_ref[...] + add_scores(me_ref[0], (low_ref, high_ref), slices_ref, step, inner)


def last_body(me_ref, low_ref, high_ref, slices_ref, sum_ref, hot_ref, wide_ref, out_ref, *, step, inner):
    scores = sum_ref[...] + add_scores(me_ref[0], (low_ref, high_ref), slices_ref, step, inner)
    masked = 0.125 * (scores * wide_ref[...])
    high = masked.astype(jnp.bfloat16)
    low = (masked - high.astype(jnp.float32)).astype(jnp.bfloat16)
    out_ref[...] = dot(hot_ref[...], high) + dot(hot_ref[...], low)


def total_body(parts_ref, out_ref):
    kept, count = out_ref.shape
    total = jnp.sum(parts_ref[...], axis=0, keepdims=True)
    out_ref[...] = jnp.concatenate([total[:, r * count : (r + 1) * count] for r in range(kept)], axis=0)


def wide_sums(me, near, docs_in, topic_mask, membership, owner_slot, *, size):
    outer, inner = split(size)
    docs, width = docs_in.shape
    clusters = owner_slot.shape[0]
    order = jnp.argsort((me ^ (jnp.array(far_masks(size))[:, None] ^ jnp.arange(inner))).reshape(-1))
    slices = jnp.stack(near, axis=1).reshape((size,) + near[0].shape[1:])[order]
    precond = jnp.moveaxis(slices, 0, 1).reshape(-1, width)
    blocks = topic_mask.shape[0]
    mask = jnp.repeat(topic_mask.T.astype(jnp.float32), docs // blocks, axis=1)
    mask = jnp.repeat(mask, precond.shape[0] // mask.shape[0], axis=0)
    masked = 0.125 * (dot(precond, docs_in) * mask)
    by_slot = (jnp.arange(clusters)[:, None] == owner_slot[None, :]).astype(jnp.bfloat16)
    by_doc = (jnp.arange(clusters)[:, None] == membership[None, :]).astype(jnp.bfloat16)
    hot = jnp.dot(by_slot, by_doc, preferred_element_type=jnp.float32).astype(jnp.bfloat16)
    return dot(hot, masked.astype(jnp.bfloat16))


def tiled_sums(me, near, docs_low, doc_grads, topic_mask, membership, owner_slot, *, size):
    outer, inner = split(size)
    docs, width = doc_grads.shape
    clusters = owner_slot.shape[0]
    count = near[0].shape[1]
    work = dict(flops=2 * count * docs * width // inner, moved=2 * docs * width // inner)
    sums, hot, wide, docs_high = call(
        functools.partial(first_body, inner=inner),
        "scores_0",
        (
            jax.ShapeDtypeStruct((count, docs), jnp.float32),
            jax.ShapeDtypeStruct((clusters, docs), jnp.bfloat16),
            jax.ShapeDtypeStruct((count, docs), jnp.float32),
            pltpu.VMEM((docs - docs_low.shape[0], width), doc_grads.dtype),
        ),
        **work,
    )(
        in_specs=[SMEM, VMEM, HBM] + [VMEM] * 4,
        out_specs=(VMEM,) * 4,
        scratch_shapes=[pltpu.SemaphoreType.DMA((1,))],
    )(
        me,
        docs_low,
        far_memory(doc_grads),
        near[0],
        topic_mask,
        membership.reshape(1, docs),
        owner_slot.reshape(1, clusters),
    )
    near_docs = (docs_low, near_memory(docs_high))
    for t in range(1, inner - 1):
        sums = call(
            functools.partial(next_body, step=t, inner=inner),
            f"scores_{t}",
            jax.ShapeDtypeStruct((count, docs), jnp.float32),
            **work,
        )(in_specs=[SMEM] + [VMEM] * 4, out_specs=VMEM)(me, *near_docs, near[t], sums)
    return call(
        functools.partial(last_body, step=inner - 1, inner=inner),
        "sums",
        jax.ShapeDtypeStruct((clusters, count), jnp.float32),
        **work,
    )(in_specs=[SMEM] + [VMEM] * 6, out_specs=VMEM)(me, *near_docs, near[inner - 1], sums, hot, wide)


def per_device(doc_grads, val_grads, inv_hessian, topic_mask, membership, owner_slot, *, size):
    outer, inner = split(size)
    me = lax.axis_index("blk").astype(jnp.int32).reshape(1)
    docs = doc_grads.shape[0]
    val_local, width = val_grads.shape
    rows = inv_hessian.shape[0]
    clusters = owner_slot.shape[0]
    kept = clusters // size
    count = size * val_local
    masks = far_masks(size)[1:]

    far = [val_grads] + [send(val_grads, size, mask) for mask in masks]
    far[0] = fetch(val_grads, far[1])
    far = call(
        pack_body, "pack", jax.ShapeDtypeStruct((outer * val_local, width), jnp.bfloat16), 0, 4 * outer * width
    )(in_specs=[VMEM] * outer, out_specs=VMEM)(*far)
    near = [far] + [send(far, size, t) for t in range(1, inner)]
    near_hess = fetch(inv_hessian, far)
    early = docs * 3 // 4
    panel, docs_low = call(
        functools.partial(panel_body, outer=outer, inner=inner),
        "panel",
        (jax.ShapeDtypeStruct((count, rows), jnp.bfloat16), pltpu.VMEM((early, width), doc_grads.dtype)),
        2 * count * rows * width,
        2 * rows * width,
        16,
    )(
        in_specs=[SMEM] + [VMEM] * (inner + 1) + [HBM],
        out_specs=(VMEM, VMEM),
        scratch_shapes=[pltpu.SemaphoreType.DMA((1,))],
    )(me, *near, near_hess, far_memory(doc_grads))

    far = jnp.stack([panel] + [send(panel, size, mask) for mask in masks])
    near = [far] + [send(far, size, t) for t in range(1, inner)]
    if rows % 128 == 0:
        sums = tiled_sums(me, near, near_memory(docs_low), doc_grads, topic_mask, membership, owner_slot, size=size)
    else:
        sums = wide_sums(me, near, doc_grads, topic_mask, membership, owner_slot, size=size)

    sums = lax.all_to_all(sums.reshape(size, kept * count), "blk", 0, 0, tiled=True)
    return call(total_body, "total", jax.ShapeDtypeStruct((kept, count), jnp.float32), 0, 8 * size * kept * count)(
        in_specs=[VMEM], out_specs=VMEM
    )(sums)


def solution(mesh):
    size = mesh.shape["blk"]

    def run(*args):
        return per_device(*args, size=size)

    in_specs = (
        P(("grp", "blk"), None),
        P("blk", None),
        P("blk", None),
        P(("grp", "blk"), None),
        P(("grp", "blk")),
        P(),
    )
    out_specs = P(("grp", "blk"), None)
    return jax.shard_map(run, mesh=mesh, in_specs=in_specs, out_specs=out_specs, check_vma=False)
```

```python
import functools

import jax
import jax.numpy as jnp
from jax import lax
from jax.experimental import pallas as pl
from jax.experimental.pallas import tpu as pltpu
from jax.sharding import PartitionSpec as P

ROWS_BY_ROWS = (((1,), (1,)), ((), ()))
VMEM = pl.BlockSpec(memory_space=pltpu.VMEM)
HBM = pl.BlockSpec(memory_space=pltpu.HBM)
SMEM = pl.BlockSpec(memory_space=pltpu.SMEM)


def dot(a, b, dims=ROWS_BY_ROWS):
    return lax.dot_general(a, b, dims, preferred_element_type=jnp.float32)


def near_memory(x):
    return pltpu.with_memory_space_constraint(x, pltpu.VMEM)


def far_memory(x):
    return pltpu.with_memory_space_constraint(x, pltpu.HBM)


def call(body, name, out_shape, flops, moved, limit=12):
    return functools.partial(
        pl.pallas_call,
        body,
        out_shape=out_shape,
        compiler_params=pltpu.CompilerParams(vmem_limit_bytes=limit << 20),
        cost_estimate=pl.CostEstimate(flops=flops, bytes_accessed=moved, transcendentals=0),
        name=name,
    )


def send(x, size, mask):
    return lax.ppermute(x, "blk", [(i, i ^ mask) for i in range(size)])


def start_copies(ref, start, out, sems):
    pieces = sems.shape[0]
    rows = out.shape[0] // pieces
    copies = []
    for i in range(pieces):
        here, there = pl.ds(start + i * rows, rows), pl.ds(i * rows, rows)
        copies.append(pltpu.make_async_copy(ref.at[here], out.at[there], sems.at[i]))
        copies[-1].start()
    return copies


def fetch(x, after):
    def body(x_ref, _, out_ref, sems):
        for copy in start_copies(x_ref, 0, out_ref, sems):
            copy.wait()

    run = call(body, "fetch", pltpu.VMEM(x.shape, x.dtype), 0, 2 * x.size * x.dtype.itemsize, 1)(
        in_specs=[HBM, pl.BlockSpec(memory_space=pl.ANY)], out_specs=VMEM, scratch_shapes=[pltpu.SemaphoreType.DMA((1,))]
    )
    return near_memory(run(far_memory(x), after))


def split(size):
    inner = 1
    while inner * inner * 4 <= size:
        inner *= 2
    return size // inner, inner


def far_masks(size):
    outer, inner = split(size)
    return [s * inner + (s > 0 and inner > 1) for s in range(outer)]


def gather_stages(size):
    outer, inner = split(size)
    if inner < 2:
        return [[s * inner for s in range(1, outer)]]
    near = [2 * a + 1 for a in range(1, inner // 2)]
    far = [s * inner + 1 for s in range(1, outer)]
    if len(far) == 3:
        far = [far[0], far[2], far[1]]
    return [stage for stage in (near, far, [1]) if stage]


def pack_body(*refs):
    parts, out = refs[:-2], refs[-1]
    out[...] = jnp.concatenate([r[...].astype(jnp.float32) for r in parts], axis=0).astype(out.dtype)


def panel_body(me_ref, *refs, order):
    parts, hess_ref, docs_ref, out_ref, docs_out, sems = refs[:-5], *refs[-5:]
    copies = start_copies(docs_ref, 0, docs_out, sems)
    vals = jnp.concatenate([r[...].astype(jnp.float32) for r in parts], axis=0).astype(jnp.bfloat16)
    count = vals.shape[0]
    each = count // len(order)
    to = lax.broadcasted_iota(jnp.int32, (count, count), 0)
    at = lax.broadcasted_iota(jnp.int32, (count, count), 1)
    origin = jnp.zeros_like(at)
    for i, mask in enumerate(order):
        origin = jnp.where(at // each == i, mask, origin)
    place = (to == (me_ref[0] ^ origin) * each + at % each).astype(jnp.float32).astype(jnp.bfloat16)
    out_ref[...] = dot(place, dot(hess_ref[...], vals).astype(jnp.bfloat16)).astype(out_ref.dtype)
    for copy in copies:
        copy.wait()


def scores_of(me, docs_ref, slices_ref, step, inner):
    outer, _, rows = slices_ref.shape
    total = None
    for s, mask in enumerate(far_masks(outer * inner)):
        column = pl.multiple_of((me ^ mask ^ step) * rows, rows)
        part = dot(slices_ref[s], docs_ref[:, pl.ds(column, rows)])
        total = part if total is None else total + part
    return total


def add_scores(me, docs_refs, slices_ref, step, inner):
    return jnp.concatenate([scores_of(me, r, slices_ref, step, inner) for r in docs_refs], axis=1)


def first_body(
    me_ref, low_ref, docs_ref, slices_ref, mask_ref, member_ref, slot_ref, out_ref, hot_ref, wide_ref, high_ref, sems, *, inner
):
    split_at = low_ref.shape[0]
    copies = start_copies(docs_ref, split_at, high_ref, sems)
    out_ref[:, :split_at] = scores_of(me_ref[0], low_ref, slices_ref, 0, inner)
    clusters, docs = hot_ref.shape
    row = lax.broadcasted_iota(jnp.int32, (clusters, clusters), 0)
    by_slot = (row == slot_ref[...]).astype(jnp.float32).astype(jnp.bfloat16)
    cluster = lax.broadcasted_iota(jnp.int32, (clusters, docs), 0)
    by_doc = (cluster == member_ref[...]).astype(jnp.float32).astype(jnp.bfloat16)
    hot_ref[...] = dot(by_slot, by_doc, (((1,), (0,)), ((), ()))).astype(jnp.bfloat16)
    blocks = mask_ref.shape[0]
    doc = lax.broadcasted_iota(jnp.int32, (blocks, docs), 1)
    spread = (doc // (docs // blocks) == lax.broadcasted_iota(jnp.int32, (blocks, docs), 0)).astype(jnp.float32)
    narrow = mask_ref[...].astype(jnp.float32)
    wide_ref[...] = dot(narrow.astype(jnp.bfloat16), spread.astype(jnp.bfloat16), (((0,), (0,)), ((), ())))
    for copy in copies:
        copy.wait()
    out_ref[:, split_at:] = scores_of(me_ref[0], high_ref, slices_ref, 0, inner)


def next_body(me_ref, low_ref, high_ref, slices_ref, sum_ref, out_ref, *, step, inner):
    out_ref[...] = sum_ref[...] + add_scores(me_ref[0], (low_ref, high_ref), slices_ref, step, inner)


def last_body(me_ref, low_ref, high_ref, slices_ref, sum_ref, hot_ref, wide_ref, out_ref, *, step, inner):
    scores = sum_ref[...] + add_scores(me_ref[0], (low_ref, high_ref), slices_ref, step, inner)
    masked = 0.125 * (scores * wide_ref[...])
    high = masked.astype(jnp.bfloat16)
    low = (masked - high.astype(jnp.float32)).astype(jnp.bfloat16)
    out_ref[...] = dot(hot_ref[...], high) + dot(hot_ref[...], low)


def total_body(parts_ref, out_ref):
    kept, count = out_ref.shape
    total = jnp.sum(parts_ref[...], axis=0, keepdims=True)
    out_ref[...] = jnp.concatenate([total[:, r * count : (r + 1) * count] for r in range(kept)], axis=0)


def wide_sums(me, near, docs_in, topic_mask, membership, owner_slot, *, size):
    outer, inner = split(size)
    docs, width = docs_in.shape
    clusters = owner_slot.shape[0]
    order = jnp.argsort((me ^ (jnp.array(far_masks(size))[:, None] ^ jnp.arange(inner))).reshape(-1))
    slices = jnp.stack(near, axis=1).reshape((size,) + near[0].shape[1:])[order]
    precond = jnp.moveaxis(slices, 0, 1).reshape(-1, width)
    blocks = topic_mask.shape[0]
    mask = jnp.repeat(topic_mask.T.astype(jnp.float32), docs // blocks, axis=1)
    mask = jnp.repeat(mask, precond.shape[0] // mask.shape[0], axis=0)
    masked = 0.125 * (dot(precond, docs_in) * mask)
    by_slot = (jnp.arange(clusters)[:, None] == owner_slot[None, :]).astype(jnp.bfloat16)
    by_doc = (jnp.arange(clusters)[:, None] == membership[None, :]).astype(jnp.bfloat16)
    hot = jnp.dot(by_slot, by_doc, preferred_element_type=jnp.float32).astype(jnp.bfloat16)
    return dot(hot, masked.astype(jnp.bfloat16))


def tiled_sums(me, near, docs_low, doc_grads, topic_mask, membership, owner_slot, *, size):
    outer, inner = split(size)
    docs, width = doc_grads.shape
    clusters = owner_slot.shape[0]
    count = near[0].shape[1]
    work = dict(flops=2 * count * docs * width // inner, moved=2 * docs * width // inner)
    sums, hot, wide, docs_high = call(
        functools.partial(first_body, inner=inner),
        "scores_0",
        (
            jax.ShapeDtypeStruct((count, docs), jnp.float32),
            jax.ShapeDtypeStruct((clusters, docs), jnp.bfloat16),
            jax.ShapeDtypeStruct((count, docs), jnp.float32),
            pltpu.VMEM((docs - docs_low.shape[0], width), doc_grads.dtype),
        ),
        **work,
    )(
        in_specs=[SMEM, VMEM, HBM] + [VMEM] * 4,
        out_specs=(VMEM,) * 4,
        scratch_shapes=[pltpu.SemaphoreType.DMA((1,))],
    )(
        me,
        docs_low,
        far_memory(doc_grads),
        near[0],
        topic_mask,
        membership.reshape(1, docs),
        owner_slot.reshape(1, clusters),
    )
    near_docs = (docs_low, near_memory(docs_high))
    for t in range(1, inner - 1):
        sums = call(
            functools.partial(next_body, step=t, inner=inner),
            f"scores_{t}",
            jax.ShapeDtypeStruct((count, docs), jnp.float32),
            **work,
        )(in_specs=[SMEM] + [VMEM] * 4, out_specs=VMEM)(me, *near_docs, near[t], sums)
    return call(
        functools.partial(last_body, step=inner - 1, inner=inner),
        "sums",
        jax.ShapeDtypeStruct((clusters, count), jnp.float32),
        **work,
    )(in_specs=[SMEM] + [VMEM] * 6, out_specs=VMEM)(me, *near_docs, near[inner - 1], sums, hot, wide)


def per_device(doc_grads, val_grads, inv_hessian, topic_mask, membership, owner_slot, *, size):
    outer, inner = split(size)
    me = lax.axis_index("blk").astype(jnp.int32).reshape(1)
    docs = doc_grads.shape[0]
    val_local, width = val_grads.shape
    rows = inv_hessian.shape[0]
    clusters = owner_slot.shape[0]
    kept = clusters // size
    count = size * val_local
    masks = far_masks(size)[1:]

    order, held = [0], fetch(val_grads, me)
    outgoing, near_hess = val_grads, None
    stages = gather_stages(size)
    for stage in stages:
        came = [send(outgoing, size, mask) for mask in stage]
        order += [mask ^ o for mask in stage for o in order]
        if stage is stages[-2]:
            near_hess = fetch(inv_hessian, held)
        if stage is not stages[-1]:
            shape = ((len(came) + 1) * held.shape[0], width)
            held = call(pack_body, "pack", jax.ShapeDtypeStruct(shape, held.dtype), 0, 4 * shape[0] * width)(
                in_specs=[VMEM] * (len(came) + 1) + [pl.BlockSpec(memory_space=pl.ANY)], out_specs=VMEM
            )(held, *came, me if near_hess is None else near_hess)
            outgoing = held
    near = [held] + came
    early = docs * 3 // 4
    panel, docs_low = call(
        functools.partial(panel_body, order=order),
        "panel",
        (jax.ShapeDtypeStruct((count, rows), jnp.bfloat16), pltpu.VMEM((early, width), doc_grads.dtype)),
        2 * count * rows * width,
        2 * rows * width,
        16,
    )(
        in_specs=[SMEM] + [VMEM] * (len(near) + 1) + [HBM],
        out_specs=(VMEM, VMEM),
        scratch_shapes=[pltpu.SemaphoreType.DMA((1,))],
    )(me, *near, near_hess, far_memory(doc_grads))

    far = jnp.stack([panel] + [send(panel, size, mask) for mask in masks])
    near = [far] + [send(far, size, t) for t in range(1, inner)]
    if rows % 128 == 0:
        sums = tiled_sums(me, near, near_memory(docs_low), doc_grads, topic_mask, membership, owner_slot, size=size)
    else:
        sums = wide_sums(me, near, doc_grads, topic_mask, membership, owner_slot, size=size)

    sums = lax.all_to_all(sums.reshape(size, kept * count), "blk", 0, 0, tiled=True)
    return call(total_body, "total", jax.ShapeDtypeStruct((kept, count), jnp.float32), 0, 8 * size * kept * count)(
        in_specs=[VMEM], out_specs=VMEM
    )(sums)


def solution(mesh):
    size = mesh.shape["blk"]

    def run(*args):
        return per_device(*args, size=size)

    in_specs = (
        P(("grp", "blk"), None),
        P("blk", None),
        P("blk", None),
        P(("grp", "blk"), None),
        P(("grp", "blk")),
        P(),
    )
    out_specs = P(("grp", "blk"), None)
    return jax.shard_map(run, mesh=mesh, in_specs=in_specs, out_specs=out_specs, check_vma=False)
```

```python
import functools
import math

import jax
import jax.numpy as jnp
from jax import lax
from jax.experimental import pallas as pl
from jax.experimental.pallas import tpu as pltpu
from jax.sharding import PartitionSpec as P

ROWS_BY_ROWS = (((1,), (1,)), ((), ()))
VMEM = pl.BlockSpec(memory_space=pltpu.VMEM)
HBM = pl.BlockSpec(memory_space=pltpu.HBM)
SMEM = pl.BlockSpec(memory_space=pltpu.SMEM)


def dot(a, b, dims=ROWS_BY_ROWS):
    return lax.dot_general(a, b, dims, preferred_element_type=jnp.float32)


def near_memory(x):
    return pltpu.with_memory_space_constraint(x, pltpu.VMEM)


def far_memory(x):
    return pltpu.with_memory_space_constraint(x, pltpu.HBM)


def call(body, name, out_shape, flops, moved, limit=12):
    return functools.partial(
        pl.pallas_call,
        body,
        out_shape=out_shape,
        compiler_params=pltpu.CompilerParams(vmem_limit_bytes=limit << 20),
        cost_estimate=pl.CostEstimate(flops=flops, bytes_accessed=moved, transcendentals=0),
        name=name,
    )


def send(x, size, mask):
    return lax.ppermute(x, "blk", [(i, i ^ mask) for i in range(size)])


def start_copies(ref, start, out, sems):
    pieces = sems.shape[0]
    rows = out.shape[0] // pieces
    copies = []
    for i in range(pieces):
        here, there = ref, out
        if ref.shape[0] != rows:
            here, there = ref.at[pl.ds(start + i * rows, rows)], out.at[pl.ds(i * rows, rows)]
        copies.append(pltpu.make_async_copy(here, there, sems.at[i]))
        copies[-1].start()
    return copies


def fetch(x, after, first=0, count=None, into=None):
    count = x.shape[0] - first if count is None else count

    def body(x_ref, *refs):
        out_ref, sems = refs[-2:]
        part = out_ref if count == out_ref.shape[0] else out_ref.at[pl.ds(first, count)]
        for copy in start_copies(x_ref, first, part, sems):
            copy.wait()

    run = call(body, "fetch", pltpu.VMEM(x.shape, x.dtype), 0, 2 * count * x.shape[1] * x.dtype.itemsize, 1)(
        in_specs=[HBM, pl.BlockSpec(memory_space=pl.ANY)] + [VMEM] * (into is not None),
        out_specs=VMEM,
        scratch_shapes=[pltpu.SemaphoreType.DMA((1,))],
        input_output_aliases={} if into is None else {2: 0},
    )
    return near_memory(run(far_memory(x), after, *([] if into is None else [into])))


def split(size):
    inner = 1
    while inner * inner * 4 <= size:
        inner *= 2
    return size // inner, inner


def stack_body(*refs):
    parts, out = refs[:-2], refs[-1]
    for i, part in enumerate(parts):
        n = part.shape[0]
        out[i * n : (i + 1) * n] = part[...]


def gather_stages(size):
    outer, inner = split(size)
    if inner < 2:
        return [[s * inner for s in range(1, outer)]]
    near = [2 * a + 1 for a in range(1, inner // 2)]
    far = [s * inner + 1 for s in range(1, outer)]
    if len(far) == 3:
        far = [far[0], far[2], far[1]]
    return [stage for stage in (near, far, [1]) if stage]


def pack_body(*refs):
    parts, out = refs[:-2], refs[-1]
    out[...] = jnp.concatenate([r[...].astype(jnp.float32) for r in parts], axis=0).astype(out.dtype)


def panel_body(me_ref, *refs, order):
    parts, hess_ref, docs_ref, out_ref, docs_out, sems = refs[:-5], *refs[-5:]
    copies = start_copies(docs_ref, 0, docs_out, sems)
    vals = jnp.concatenate([r[...].astype(jnp.float32) for r in parts], axis=0).astype(jnp.bfloat16)
    count = vals.shape[0]
    each = count // len(order)
    to = lax.broadcasted_iota(jnp.int32, (count, count), 0)
    at = lax.broadcasted_iota(jnp.int32, (count, count), 1)
    origin = jnp.zeros_like(at)
    for i, mask in enumerate(order):
        origin = jnp.where(at // each == i, mask, origin)
    place = (to == (me_ref[0] ^ origin) * each + at % each).astype(jnp.float32).astype(jnp.bfloat16)
    out_ref[...] = dot(place, dot(hess_ref[...], vals).astype(jnp.bfloat16)).astype(out_ref.dtype)
    for copy in copies:
        copy.wait()


def scores_of(me, docs_ref, parts):
    total = None
    for slices_ref, masks in parts:
        rows = slices_ref.shape[-1]
        for s, mask in enumerate(masks):
            column = pl.multiple_of((me ^ mask) * rows, rows)
            part = dot(slices_ref[s], docs_ref[:, pl.ds(column, rows)])
            total = part if total is None else total + part
    return total


def add_scores(me, docs_refs, parts):
    return jnp.concatenate([scores_of(me, r, parts) for r in docs_refs], axis=1)


def first_body(me_ref, low_ref, docs_ref, mask_ref, member_ref, slot_ref, *refs, masks, size):
    parts = list(zip(refs[: len(masks)], masks))
    out_ref, hot_ref, wide_ref, high_ref, sems = refs[len(masks) :]
    split_at = low_ref.shape[0]
    copies = start_copies(docs_ref, split_at, high_ref, sems)
    out_ref[:, :split_at] = scores_of(me_ref[0], low_ref, parts)
    clusters, docs = hot_ref.shape
    row = lax.broadcasted_iota(jnp.int32, (clusters, clusters), 0)
    kept = clusters // size
    slot = (size - 1 - row // kept) * kept + row % kept
    by_slot = (slot == slot_ref[...]).astype(jnp.float32).astype(jnp.bfloat16)
    cluster = lax.broadcasted_iota(jnp.int32, (clusters, docs), 0)
    by_doc = (cluster == member_ref[...]).astype(jnp.float32).astype(jnp.bfloat16)
    hot_ref[...] = dot(by_slot, by_doc, (((1,), (0,)), ((), ()))).astype(jnp.bfloat16)
    blocks = mask_ref.shape[0]
    doc = lax.broadcasted_iota(jnp.int32, (blocks, docs), 1)
    spread = (doc // (docs // blocks) == lax.broadcasted_iota(jnp.int32, (blocks, docs), 0)).astype(jnp.float32)
    narrow = mask_ref[...].astype(jnp.float32)
    wide_ref[...] = dot(narrow.astype(jnp.bfloat16), spread.astype(jnp.bfloat16), (((0,), (0,)), ((), ())))
    for copy in copies:
        copy.wait()
    out_ref[:, split_at:] = scores_of(me_ref[0], high_ref, parts)


def next_body(me_ref, low_ref, high_ref, sum_ref, *refs, masks):
    parts = list(zip(refs, masks))
    refs[-1][...] = sum_ref[...] + add_scores(me_ref[0], (low_ref, high_ref), parts)


def last_body(me_ref, low_ref, high_ref, sum_ref, hot_ref, wide_ref, *refs, masks):
    parts, out_ref = list(zip(refs, masks)), refs[-1]
    scores = sum_ref[...] + add_scores(me_ref[0], (low_ref, high_ref), parts)
    masked = 0.125 * (scores * wide_ref[...])
    high = masked.astype(jnp.bfloat16)
    low = (masked - high.astype(jnp.float32)).astype(jnp.bfloat16)
    out_ref[...] = dot(hot_ref[...], high) + dot(hot_ref[...], low)


def total_body(parts_ref, out_ref):
    kept, count = out_ref.shape
    total = jnp.sum(parts_ref[...], axis=0, keepdims=True)
    out_ref[...] = jnp.concatenate([total[:, r * count : (r + 1) * count] for r in range(kept)], axis=0)


def wide_sums(me, own, came, docs_in, topic_mask, membership, owner_slot, *, size):
    docs, width = docs_in.shape
    clusters = owner_slot.shape[0]
    arrays, masks = zip(own, *came)
    held, masks = jnp.concatenate(arrays), sum(masks, [])
    slices = jnp.concatenate([held, send(held, size, 1)])
    origins = me ^ jnp.array(masks + [mask ^ 1 for mask in masks])
    precond = jnp.moveaxis(slices[jnp.argsort(origins)], 0, 1).reshape(-1, width)
    blocks = topic_mask.shape[0]
    mask = jnp.repeat(topic_mask.T.astype(jnp.float32), docs // blocks, axis=1)
    mask = jnp.repeat(mask, precond.shape[0] // mask.shape[0], axis=0)
    masked = 0.125 * (dot(precond, docs_in) * mask)
    slot = jnp.arange(clusters).reshape(size, -1)[::-1].reshape(-1)
    by_slot = (slot[:, None] == owner_slot[None, :]).astype(jnp.bfloat16)
    by_doc = (jnp.arange(clusters)[:, None] == membership[None, :]).astype(jnp.bfloat16)
    hot = jnp.dot(by_slot, by_doc, preferred_element_type=jnp.float32).astype(jnp.bfloat16)
    return dot(hot, masked.astype(jnp.bfloat16))


def tiled_sums(me, own, came, docs_low, doc_grads, topic_mask, membership, owner_slot, *, size):
    docs, width = doc_grads.shape
    clusters = owner_slot.shape[0]
    count = own[0].shape[1]

    def run(body, name, out_shape, step, operands, in_specs, **more):
        arrays, masks = zip(*step)
        share = sum(len(m) for m in masks) * docs * width // size
        out_specs = (VMEM,) * len(out_shape) if isinstance(out_shape, tuple) else VMEM
        return call(functools.partial(body, masks=masks), name, out_shape, 2 * count * share, 2 * share)(
            in_specs=in_specs + [VMEM] * len(arrays), out_specs=out_specs, **more
        )(*operands, *arrays)

    total = jax.ShapeDtypeStruct((count, docs), jnp.float32)
    sums, hot, wide, docs_high = run(
        functools.partial(first_body, size=size),
        "scores_first",
        (
            total,
            jax.ShapeDtypeStruct((clusters, docs), jnp.bfloat16),
            total,
            pltpu.VMEM((docs - docs_low.shape[0], width), doc_grads.dtype),
        ),
        [own],
        (me, docs_low, far_memory(doc_grads), topic_mask, membership.reshape(1, docs), owner_slot.reshape(1, clusters)),
        [SMEM, VMEM, HBM] + [VMEM] * 3,
        scratch_shapes=[pltpu.SemaphoreType.DMA((1,))],
    )
    both = (docs_low, near_memory(docs_high))
    arrays, masks = zip(own, *came)
    shape = (sum(a.shape[0] for a in arrays),) + arrays[0].shape[1:]
    held = call(stack_body, "stack", jax.ShapeDtypeStruct(shape, arrays[0].dtype), 0, 4 * math.prod(shape))(
        in_specs=[VMEM] * len(arrays) + [pl.BlockSpec(memory_space=pl.ANY)], out_specs=VMEM
    )(*arrays, sums)
    other = (send(held, size, 1), [mask ^ 1 for mask in sum(masks, [])])
    sums = run(next_body, "scores_next", total, came, (me, *both, sums), [SMEM] + [VMEM] * 3)
    shape = jax.ShapeDtypeStruct((clusters, count), jnp.float32)
    return run(last_body, "sums", shape, [other], (me, *both, sums, hot, wide), [SMEM] + [VMEM] * 5)


def per_device(doc_grads, val_grads, inv_hessian, topic_mask, membership, owner_slot, *, size):
    outer, inner = split(size)
    me = lax.axis_index("blk").astype(jnp.int32).reshape(1)
    docs = doc_grads.shape[0]
    val_local, width = val_grads.shape
    rows = inv_hessian.shape[0]
    clusters = owner_slot.shape[0]
    kept = clusters // size
    count = size * val_local
    order, held = [0], fetch(val_grads, me)
    outgoing, near_hess = val_grads, None
    stages = gather_stages(size)
    for k, stage in enumerate(stages):
        came = [send(outgoing, size, mask) for mask in stage]
        order += [mask ^ o for mask in stage for o in order]
        if k < 2:
            near_hess = fetch(inv_hessian, held, k * (rows // 2), rows // 2, into=near_hess)
        if stage is not stages[-1]:
            shape = ((len(came) + 1) * held.shape[0], width)
            held = call(pack_body, "pack", jax.ShapeDtypeStruct(shape, held.dtype), 0, 4 * shape[0] * width)(
                in_specs=[VMEM] * (len(came) + 1) + [pl.BlockSpec(memory_space=pl.ANY)], out_specs=VMEM
            )(held, *came, me if near_hess is None else near_hess)
            outgoing = held
    near = [held] + came
    early = docs * 5 // 8
    panel, docs_low = call(
        functools.partial(panel_body, order=order),
        "panel",
        (jax.ShapeDtypeStruct((count, rows), jnp.bfloat16), pltpu.VMEM((early, width), doc_grads.dtype)),
        2 * count * rows * width,
        2 * rows * width,
        16,
    )(
        in_specs=[SMEM] + [VMEM] * (len(near) + 1) + [HBM],
        out_specs=(VMEM, VMEM),
        scratch_shapes=[pltpu.SemaphoreType.DMA((1,))],
    )(me, *near, near_hess, far_memory(doc_grads))

    near, far, _ = stages
    own = jnp.stack([panel] + [send(panel, size, mask) for mask in near])
    own_masks = [0] + near
    came = [(send(own, size, mask), [mask ^ m for m in own_masks]) for mask in far]

    find = tiled_sums if rows % 128 == 0 else wide_sums
    given = (near_memory(docs_low), doc_grads) if rows % 128 == 0 else (doc_grads,)
    sums = find(me, (own, own_masks), came, *given, topic_mask, membership, owner_slot, size=size)

    backwards = list(range(size - 1, -1, -1))
    sums = lax.all_to_all(sums.reshape(size, kept * count), "blk", 0, 0, tiled=True, axis_index_groups=[backwards])
    return call(total_body, "total", jax.ShapeDtypeStruct((kept, count), jnp.float32), 0, 8 * size * kept * count)(
        in_specs=[VMEM], out_specs=VMEM
    )(sums)


def solution(mesh):
    size = mesh.shape["blk"]

    def run(*args):
        return per_device(*args, size=size)

    in_specs = (
        P(("grp", "blk"), None),
        P("blk", None),
        P("blk", None),
        P(("grp", "blk"), None),
        P(("grp", "blk")),
        P(),
    )
    out_specs = P(("grp", "blk"), None)
    return jax.shard_map(run, mesh=mesh, in_specs=in_specs, out_specs=out_specs, check_vma=False)
```

```python
import functools
import math

import jax
import jax.numpy as jnp
from jax import lax
from jax.experimental import pallas as pl
from jax.experimental.pallas import tpu as pltpu
from jax.sharding import PartitionSpec as P

ROWS_BY_ROWS = (((1,), (1,)), ((), ()))
VMEM = pl.BlockSpec(memory_space=pltpu.VMEM)
HBM = pl.BlockSpec(memory_space=pltpu.HBM)
SMEM = pl.BlockSpec(memory_space=pltpu.SMEM)


def dot(a, b, dims=ROWS_BY_ROWS):
    return lax.dot_general(a, b, dims, preferred_element_type=jnp.float32)


def near_memory(x):
    return pltpu.with_memory_space_constraint(x, pltpu.VMEM)


def far_memory(x):
    return pltpu.with_memory_space_constraint(x, pltpu.HBM)


def call(body, name, out_shape, flops, moved, limit=12):
    return functools.partial(
        pl.pallas_call,
        body,
        out_shape=out_shape,
        compiler_params=pltpu.CompilerParams(vmem_limit_bytes=limit << 20),
        cost_estimate=pl.CostEstimate(flops=flops, bytes_accessed=moved, transcendentals=0),
        name=name,
    )


def send(x, size, mask):
    return lax.ppermute(x, "blk", [(i, i ^ mask) for i in range(size)])


def start_copies(ref, start, out, sems):
    pieces = sems.shape[0]
    rows = out.shape[0] // pieces
    copies = []
    for i in range(pieces):
        here, there = ref, out
        if ref.shape[0] != rows:
            here, there = ref.at[pl.ds(start + i * rows, rows)], out.at[pl.ds(i * rows, rows)]
        copies.append(pltpu.make_async_copy(here, there, sems.at[i]))
        copies[-1].start()
    return copies


def fetch(x, after, first=0, count=None, into=None):
    count = x.shape[0] - first if count is None else count

    def body(x_ref, *refs):
        out_ref, sems = refs[-2:]
        part = out_ref if count == out_ref.shape[0] else out_ref.at[pl.ds(first, count)]
        for copy in start_copies(x_ref, first, part, sems):
            copy.wait()

    run = call(body, "fetch", pltpu.VMEM(x.shape, x.dtype), 0, 2 * count * x.shape[1] * x.dtype.itemsize, 1)(
        in_specs=[HBM, pl.BlockSpec(memory_space=pl.ANY)] + [VMEM] * (into is not None),
        out_specs=VMEM,
        scratch_shapes=[pltpu.SemaphoreType.DMA((1,))],
        input_output_aliases={} if into is None else {2: 0},
    )
    return near_memory(run(far_memory(x), after, *([] if into is None else [into])))


def split(size):
    inner = 1
    while inner * inner * 4 <= size:
        inner *= 2
    return size // inner, inner


def stack_body(*refs):
    parts, out = refs[:-2], refs[-1]
    for i, part in enumerate(parts):
        n = part.shape[0]
        out[i * n : (i + 1) * n] = part[...]


def gather_stages(size):
    outer, inner = split(size)
    if inner < 2:
        return [[s * inner for s in range(1, outer)]]
    near = [2 * a + 1 for a in range(1, inner // 2)]
    far = [s * inner + 1 for s in range(1, outer)]
    if len(far) == 3:
        far = [far[0], far[2], far[1]]
    return [stage for stage in (near, far, [1]) if stage]


def pack_body(*refs):
    parts, out = refs[:-2], refs[-1]
    out[...] = jnp.concatenate([r[...].astype(jnp.float32) for r in parts], axis=0).astype(out.dtype)


def panel_body(me_ref, *refs, order):
    parts, hess_ref, docs_ref, out_ref, docs_out, sems = refs[:-5], *refs[-5:]
    copies = start_copies(docs_ref, 0, docs_out, sems)
    vals = jnp.concatenate([r[...].astype(jnp.float32) for r in parts], axis=0).astype(jnp.bfloat16)
    count = vals.shape[0]
    each = count // len(order)
    to = lax.broadcasted_iota(jnp.int32, (count, count), 0)
    at = lax.broadcasted_iota(jnp.int32, (count, count), 1)
    origin = jnp.zeros_like(at)
    for i, mask in enumerate(order):
        origin = jnp.where(at // each == i, mask, origin)
    place = (to == (me_ref[0] ^ origin) * each + at % each).astype(jnp.float32).astype(jnp.bfloat16)
    out_ref[...] = dot(place, dot(hess_ref[...], vals).astype(jnp.bfloat16)).astype(out_ref.dtype)
    for copy in copies:
        copy.wait()


def scores_of(me, docs_ref, parts):
    total = None
    for slices_ref, masks in parts:
        rows = slices_ref.shape[-1]
        for s, mask in enumerate(masks):
            column = pl.multiple_of((me ^ mask) * rows, rows)
            part = dot(slices_ref[s], docs_ref[:, pl.ds(column, rows)])
            total = part if total is None else total + part
    return total


def add_scores(me, docs_refs, parts):
    return jnp.concatenate([scores_of(me, r, parts) for r in docs_refs], axis=1)


def kept_by(size):
    outer, inner = split(size)
    groups = [*range(outer - 2, 0, -1), outer - 1, 0]
    return [g * inner + i for g in groups for i in range(inner - 1, -1, -1)]


def first_body(me_ref, low_ref, docs_ref, mask_ref, member_ref, slot_ref, *refs, masks, size):
    parts = list(zip(refs[: len(masks)], masks))
    out_ref, hot_ref, wide_ref, high_ref, sems = refs[len(masks) :]
    split_at = low_ref.shape[0]
    copies = start_copies(docs_ref, split_at, high_ref, sems)
    out_ref[:, :split_at] = scores_of(me_ref[0], low_ref, parts)
    clusters, docs = hot_ref.shape
    row = lax.broadcasted_iota(jnp.int32, (clusters, clusters), 0)
    kept = clusters // size
    owner = jnp.zeros_like(row)
    for i, device in enumerate(kept_by(size)):
        owner = jnp.where(row // kept == i, device, owner)
    slot = owner * kept + row % kept
    by_slot = (slot == slot_ref[...]).astype(jnp.float32).astype(jnp.bfloat16)
    cluster = lax.broadcasted_iota(jnp.int32, (clusters, docs), 0)
    by_doc = (cluster == member_ref[...]).astype(jnp.float32).astype(jnp.bfloat16)
    hot_ref[...] = dot(by_slot, by_doc, (((1,), (0,)), ((), ()))).astype(jnp.bfloat16)
    blocks = mask_ref.shape[0]
    doc = lax.broadcasted_iota(jnp.int32, (blocks, docs), 1)
    spread = (doc // (docs // blocks) == lax.broadcasted_iota(jnp.int32, (blocks, docs), 0)).astype(jnp.float32)
    narrow = mask_ref[...].astype(jnp.float32)
    wide_ref[...] = dot(narrow.astype(jnp.bfloat16), spread.astype(jnp.bfloat16), (((0,), (0,)), ((), ())))
    for copy in copies:
        copy.wait()
    out_ref[:, split_at:] = scores_of(me_ref[0], high_ref, parts)


def next_body(me_ref, low_ref, high_ref, sum_ref, *refs, masks):
    parts = list(zip(refs, masks))
    refs[-1][...] = sum_ref[...] + add_scores(me_ref[0], (low_ref, high_ref), parts)


def last_body(me_ref, low_ref, high_ref, sum_ref, hot_ref, wide_ref, *refs, masks):
    parts, out_ref = list(zip(refs, masks)), refs[-1]
    scores = sum_ref[...] + add_scores(me_ref[0], (low_ref, high_ref), parts)
    masked = 0.125 * (scores * wide_ref[...])
    high = masked.astype(jnp.bfloat16)
    low = (masked - high.astype(jnp.float32)).astype(jnp.bfloat16)
    out_ref[...] = dot(hot_ref[...], high) + dot(hot_ref[...], low)


def total_body(parts_ref, out_ref):
    kept, count = out_ref.shape
    total = jnp.sum(parts_ref[...], axis=0, keepdims=True)
    out_ref[...] = jnp.concatenate([total[:, r * count : (r + 1) * count] for r in range(kept)], axis=0)


def wide_sums(me, own, came, docs_in, topic_mask, membership, owner_slot, *, size):
    docs, width = docs_in.shape
    clusters = owner_slot.shape[0]
    arrays, masks = zip(own, *came)
    held, masks = jnp.concatenate(arrays), sum(masks, [])
    slices = jnp.concatenate([held, send(held, size, 1)])
    origins = me ^ jnp.array(masks + [mask ^ 1 for mask in masks])
    precond = jnp.moveaxis(slices[jnp.argsort(origins)], 0, 1).reshape(-1, width)
    blocks = topic_mask.shape[0]
    mask = jnp.repeat(topic_mask.T.astype(jnp.float32), docs // blocks, axis=1)
    mask = jnp.repeat(mask, precond.shape[0] // mask.shape[0], axis=0)
    masked = 0.125 * (dot(precond, docs_in) * mask)
    slot = jnp.arange(clusters).reshape(size, -1)[jnp.array(kept_by(size))].reshape(-1)
    by_slot = (slot[:, None] == owner_slot[None, :]).astype(jnp.bfloat16)
    by_doc = (jnp.arange(clusters)[:, None] == membership[None, :]).astype(jnp.bfloat16)
    hot = jnp.dot(by_slot, by_doc, preferred_element_type=jnp.float32).astype(jnp.bfloat16)
    return dot(hot, masked.astype(jnp.bfloat16))


def tiled_sums(me, own, came, docs_low, doc_grads, topic_mask, membership, owner_slot, *, size):
    docs, width = doc_grads.shape
    clusters = owner_slot.shape[0]
    count = own[0].shape[1]

    def run(body, name, out_shape, step, operands, in_specs, **more):
        arrays, masks = zip(*step)
        share = sum(len(m) for m in masks) * docs * width // size
        out_specs = (VMEM,) * len(out_shape) if isinstance(out_shape, tuple) else VMEM
        return call(functools.partial(body, masks=masks), name, out_shape, 2 * count * share, 2 * share)(
            in_specs=in_specs + [VMEM] * len(arrays), out_specs=out_specs, **more
        )(*operands, *arrays)

    total = jax.ShapeDtypeStruct((count, docs), jnp.float32)
    sums, hot, wide, docs_high = run(
        functools.partial(first_body, size=size),
        "scores_first",
        (
            total,
            jax.ShapeDtypeStruct((clusters, docs), jnp.bfloat16),
            total,
            pltpu.VMEM((docs - docs_low.shape[0], width), doc_grads.dtype),
        ),
        [own, (send(own[0], size, 1), [mask ^ 1 for mask in own[1]])],
        (me, docs_low, far_memory(doc_grads), topic_mask, membership.reshape(1, docs), owner_slot.reshape(1, clusters)),
        [SMEM, VMEM, HBM] + [VMEM] * 3,
        scratch_shapes=[pltpu.SemaphoreType.DMA((1,))],
    )
    both = (docs_low, near_memory(docs_high))
    arrays, masks = zip(*came)
    shape = (sum(a.shape[0] for a in arrays),) + arrays[0].shape[1:]
    held = call(stack_body, "stack", jax.ShapeDtypeStruct(shape, arrays[0].dtype), 0, 4 * math.prod(shape))(
        in_specs=[VMEM] * len(arrays) + [pl.BlockSpec(memory_space=pl.ANY)], out_specs=VMEM
    )(*arrays, sums)
    other = (send(held, size, 1), [mask ^ 1 for mask in sum(masks, [])])
    sums = run(next_body, "scores_next", total, came, (me, *both, sums), [SMEM] + [VMEM] * 3)
    shape = jax.ShapeDtypeStruct((clusters, count), jnp.float32)
    return run(last_body, "sums", shape, [other], (me, *both, sums, hot, wide), [SMEM] + [VMEM] * 5)


def per_device(doc_grads, val_grads, inv_hessian, topic_mask, membership, owner_slot, *, size):
    outer, inner = split(size)
    me = lax.axis_index("blk").astype(jnp.int32).reshape(1)
    docs = doc_grads.shape[0]
    val_local, width = val_grads.shape
    rows = inv_hessian.shape[0]
    clusters = owner_slot.shape[0]
    kept = clusters // size
    count = size * val_local
    half = rows // 2

    def both_body(val_ref, hess_ref, _, val_out, hess_out, sems):
        part = pl.ds(0, half)
        copies = [
            pltpu.make_async_copy(val_ref, val_out, sems.at[0]),
            pltpu.make_async_copy(hess_ref.at[part], hess_out.at[part], sems.at[1]),
        ]
        for copy in copies:
            copy.start()
        for copy in copies:
            copy.wait()

    shapes = tuple(pltpu.VMEM(x.shape, x.dtype) for x in (val_grads, inv_hessian))
    held, near_hess = call(both_body, "fetch", shapes, 0, 2 * rows * width, 1)(
        in_specs=[HBM, HBM, pl.BlockSpec(memory_space=pl.ANY)],
        out_specs=(VMEM, VMEM),
        scratch_shapes=[pltpu.SemaphoreType.DMA((2,))],
    )(far_memory(val_grads), far_memory(inv_hessian), me)
    held, near_hess = near_memory(held), near_memory(near_hess)
    order, outgoing = [0], val_grads
    stages = gather_stages(size)
    for k, stage in enumerate(stages):
        came = [send(outgoing, size, mask) for mask in stage]
        order += [mask ^ o for mask in stage for o in order]
        if k == 1:
            near_hess = fetch(inv_hessian, held, half, rows - half, into=near_hess)
        if stage is not stages[-1]:
            shape = ((len(came) + 1) * held.shape[0], width)
            held = call(pack_body, "pack", jax.ShapeDtypeStruct(shape, held.dtype), 0, 4 * shape[0] * width)(
                in_specs=[VMEM] * (len(came) + 1) + [pl.BlockSpec(memory_space=pl.ANY)], out_specs=VMEM
            )(held, *came, me if near_hess is None else near_hess)
            outgoing = held
    near = [held] + came
    early = docs * 5 // 8
    panel, docs_low = call(
        functools.partial(panel_body, order=order),
        "panel",
        (jax.ShapeDtypeStruct((count, rows), jnp.bfloat16), pltpu.VMEM((early, width), doc_grads.dtype)),
        2 * count * rows * width,
        2 * rows * width,
        16,
    )(
        in_specs=[SMEM] + [VMEM] * (len(near) + 1) + [HBM],
        out_specs=(VMEM, VMEM),
        scratch_shapes=[pltpu.SemaphoreType.DMA((1,))],
    )(me, *near, near_hess, far_memory(doc_grads))

    near, far, _ = stages
    own = jnp.stack([panel] + [send(panel, size, mask) for mask in near])
    own_masks = [0] + near
    came = [(send(own, size, mask), [mask ^ m for m in own_masks]) for mask in far]

    find = tiled_sums if rows % 128 == 0 else wide_sums
    given = (near_memory(docs_low), doc_grads) if rows % 128 == 0 else (doc_grads,)
    sums = find(me, (own, own_masks), came, *given, topic_mask, membership, owner_slot, size=size)

    sums = lax.all_to_all(sums.reshape(size, kept * count), "blk", 0, 0, tiled=True, axis_index_groups=[kept_by(size)])
    return call(total_body, "total", jax.ShapeDtypeStruct((kept, count), jnp.float32), 0, 8 * size * kept * count)(
        in_specs=[VMEM], out_specs=VMEM
    )(sums)


def solution(mesh):
    size = mesh.shape["blk"]

    def run(*args):
        return per_device(*args, size=size)

    in_specs = (
        P(("grp", "blk"), None),
        P("blk", None),
        P("blk", None),
        P(("grp", "blk"), None),
        P(("grp", "blk")),
        P(),
    )
    out_specs = P(("grp", "blk"), None)
    return jax.shard_map(run, mesh=mesh, in_specs=in_specs, out_specs=out_specs, check_vma=False)
```

```python
import functools
import math

import jax
import jax.numpy as jnp
from jax import lax
from jax.experimental import pallas as pl
from jax.experimental.pallas import tpu as pltpu
from jax.sharding import PartitionSpec as P

ROWS_BY_ROWS = (((1,), (1,)), ((), ()))
VMEM = pl.BlockSpec(memory_space=pltpu.VMEM)
HBM = pl.BlockSpec(memory_space=pltpu.HBM)
SMEM = pl.BlockSpec(memory_space=pltpu.SMEM)


def dot(a, b, dims=ROWS_BY_ROWS):
    return lax.dot_general(a, b, dims, preferred_element_type=jnp.float32)


def near_memory(x):
    return pltpu.with_memory_space_constraint(x, pltpu.VMEM)


def far_memory(x):
    return pltpu.with_memory_space_constraint(x, pltpu.HBM)


def call(body, name, out_shape, flops, moved, limit=12):
    return functools.partial(
        pl.pallas_call,
        body,
        out_shape=out_shape,
        compiler_params=pltpu.CompilerParams(vmem_limit_bytes=limit << 20),
        cost_estimate=pl.CostEstimate(flops=flops, bytes_accessed=moved, transcendentals=0),
        name=name,
    )


def send(x, size, mask):
    return lax.ppermute(x, "blk", [(i, i ^ mask) for i in range(size)])


def start_copies(ref, start, out, sems):
    pieces = sems.shape[0]
    rows = out.shape[0] // pieces
    copies = []
    for i in range(pieces):
        here, there = ref, out
        if ref.shape[0] != rows:
            here, there = ref.at[pl.ds(start + i * rows, rows)], out.at[pl.ds(i * rows, rows)]
        copies.append(pltpu.make_async_copy(here, there, sems.at[i]))
        copies[-1].start()
    return copies


def fetch(x, after, first=0, count=None, into=None):
    count = x.shape[0] - first if count is None else count

    def body(x_ref, *refs):
        out_ref, sems = refs[-2:]
        part = out_ref if count == out_ref.shape[0] else out_ref.at[pl.ds(first, count)]
        for copy in start_copies(x_ref, first, part, sems):
            copy.wait()

    run = call(body, "fetch", pltpu.VMEM(x.shape, x.dtype), 0, 2 * count * x.shape[1] * x.dtype.itemsize, 1)(
        in_specs=[HBM, pl.BlockSpec(memory_space=pl.ANY)] + [VMEM] * (into is not None),
        out_specs=VMEM,
        scratch_shapes=[pltpu.SemaphoreType.DMA((1,))],
        input_output_aliases={} if into is None else {2: 0},
    )
    return near_memory(run(far_memory(x), after, *([] if into is None else [into])))


def split(size):
    inner = 1
    while inner * inner * 4 <= size:
        inner *= 2
    return size // inner, inner


def stack_body(*refs):
    parts, out = refs[:-2], refs[-1]
    for i, part in enumerate(parts):
        n = part.shape[0]
        out[i * n : (i + 1) * n] = part[...]


def gather_stages(size):
    outer, inner = split(size)
    if inner < 2:
        return [[s * inner for s in range(1, outer)]]
    near = [2 * a + 1 for a in range(1, inner // 2)]
    far = [s * inner + 1 for s in range(1, outer)]
    if len(far) == 3:
        far = [far[0], far[2], far[1]]
    return [stage for stage in (near, far, [1]) if stage]


def pack_body(*refs):
    parts, out = refs[:-2], refs[-1]
    out[...] = jnp.concatenate([r[...].astype(jnp.float32) for r in parts], axis=0).astype(out.dtype)


def panel_body(me_ref, *refs, order):
    parts, hess_ref, docs_ref, out_ref, docs_out, sems = refs[:-5], *refs[-5:]
    copies = start_copies(docs_ref, 0, docs_out, sems)
    vals = jnp.concatenate([r[...].astype(jnp.float32) for r in parts], axis=0).astype(jnp.bfloat16)
    count = vals.shape[0]
    each = count // len(order)
    to = lax.broadcasted_iota(jnp.int32, (count, count), 0)
    at = lax.broadcasted_iota(jnp.int32, (count, count), 1)
    origin = jnp.zeros_like(at)
    for i, mask in enumerate(order):
        origin = jnp.where(at // each == i, mask, origin)
    place = (to == (me_ref[0] ^ origin) * each + at % each).astype(jnp.float32).astype(jnp.bfloat16)
    out_ref[...] = dot(place, dot(hess_ref[...], vals).astype(jnp.bfloat16)).astype(out_ref.dtype)
    for copy in copies:
        copy.wait()


def scores_of(me, docs_ref, parts):
    total = None
    for slices_ref, masks in parts:
        rows = slices_ref.shape[-1]
        for s, mask in enumerate(masks):
            column = pl.multiple_of((me ^ mask) * rows, rows)
            part = dot(slices_ref[s], docs_ref[:, pl.ds(column, rows)])
            total = part if total is None else total + part
    return total


def add_scores(me, docs_refs, parts):
    return jnp.concatenate([scores_of(me, r, parts) for r in docs_refs], axis=1)


def kept_by(size):
    outer, inner = split(size)
    groups = [*range(outer - 2, 0, -1), outer - 1, 0]
    return [g * inner + i for g in groups for i in range(inner - 1, -1, -1)]


def first_body(me_ref, low_ref, docs_ref, mask_ref, member_ref, slot_ref, *refs, masks, size):
    parts = list(zip(refs[: len(masks)], masks))
    out_ref, hot_ref, wide_ref, high_ref, sems = refs[len(masks) :]
    split_at = low_ref.shape[0]
    copies = start_copies(docs_ref, split_at, high_ref, sems)
    out_ref[:, :split_at] = scores_of(me_ref[0], low_ref, parts)
    clusters, docs = hot_ref.shape
    row = lax.broadcasted_iota(jnp.int32, (clusters, clusters), 0)
    kept = clusters // size
    owner = jnp.zeros_like(row)
    for i, device in enumerate(kept_by(size)):
        owner = jnp.where(row % size == i, device, owner)
    slot = owner * kept + row // size
    by_slot = (slot == slot_ref[...]).astype(jnp.float32).astype(jnp.bfloat16)
    cluster = lax.broadcasted_iota(jnp.int32, (clusters, docs), 0)
    by_doc = (cluster == member_ref[...]).astype(jnp.float32).astype(jnp.bfloat16)
    hot_ref[...] = dot(by_slot, by_doc, (((1,), (0,)), ((), ()))).astype(jnp.bfloat16)
    blocks = mask_ref.shape[0]
    doc = lax.broadcasted_iota(jnp.int32, (blocks, docs), 1)
    spread = (doc // (docs // blocks) == lax.broadcasted_iota(jnp.int32, (blocks, docs), 0)).astype(jnp.float32)
    narrow = mask_ref[...].astype(jnp.float32)
    wide_ref[...] = dot(narrow.astype(jnp.bfloat16), spread.astype(jnp.bfloat16), (((0,), (0,)), ((), ())))
    for copy in copies:
        copy.wait()
    out_ref[:, split_at:] = scores_of(me_ref[0], high_ref, parts)


def next_body(me_ref, low_ref, high_ref, sum_ref, *refs, masks):
    parts = list(zip(refs, masks))
    refs[-1][...] = sum_ref[...] + add_scores(me_ref[0], (low_ref, high_ref), parts)


def last_body(me_ref, low_ref, high_ref, sum_ref, hot_ref, wide_ref, *refs, masks):
    parts, out_ref = list(zip(refs, masks)), refs[-1]
    scores = sum_ref[...] + add_scores(me_ref[0], (low_ref, high_ref), parts)
    masked = 0.125 * (scores * wide_ref[...])
    high = masked.astype(jnp.bfloat16)
    low = (masked - high.astype(jnp.float32)).astype(jnp.bfloat16)
    both = dot(hot_ref[...], jnp.concatenate([high, low], axis=0))
    both = both[:, : high.shape[0]] + both[:, high.shape[0] :]
    size = out_ref.shape[0]
    out_ref[...] = jnp.concatenate([both[r : r + size] for r in range(0, both.shape[0], size)], axis=1)


def total_body(parts_ref, out_ref):
    kept, count = out_ref.shape
    total = jnp.sum(parts_ref[...], axis=0, keepdims=True)
    out_ref[...] = jnp.concatenate([total[:, r * count : (r + 1) * count] for r in range(kept)], axis=0)


def wide_sums(me, own, came, docs_in, topic_mask, membership, owner_slot, *, size):
    docs, width = docs_in.shape
    clusters = owner_slot.shape[0]
    arrays, masks = zip(own, *came)
    held, masks = jnp.concatenate(arrays), sum(masks, [])
    slices = jnp.concatenate([held, send(held, size, 1)])
    origins = me ^ jnp.array(masks + [mask ^ 1 for mask in masks])
    precond = jnp.moveaxis(slices[jnp.argsort(origins)], 0, 1).reshape(-1, width)
    blocks = topic_mask.shape[0]
    mask = jnp.repeat(topic_mask.T.astype(jnp.float32), docs // blocks, axis=1)
    mask = jnp.repeat(mask, precond.shape[0] // mask.shape[0], axis=0)
    masked = 0.125 * (dot(precond, docs_in) * mask)
    slot = jnp.arange(clusters).reshape(size, -1)[jnp.array(kept_by(size))].reshape(-1)
    by_slot = (slot[:, None] == owner_slot[None, :]).astype(jnp.bfloat16)
    by_doc = (jnp.arange(clusters)[:, None] == membership[None, :]).astype(jnp.bfloat16)
    hot = jnp.dot(by_slot, by_doc, preferred_element_type=jnp.float32).astype(jnp.bfloat16)
    return dot(hot, masked.astype(jnp.bfloat16))


def tiled_sums(me, own, came, docs_low, doc_grads, topic_mask, membership, owner_slot, *, size):
    docs, width = doc_grads.shape
    clusters = owner_slot.shape[0]
    count = own[0].shape[1]

    def run(body, name, out_shape, step, operands, in_specs, **more):
        arrays, masks = zip(*step)
        share = sum(len(m) for m in masks) * docs * width // size
        out_specs = (VMEM,) * len(out_shape) if isinstance(out_shape, tuple) else VMEM
        return call(functools.partial(body, masks=masks), name, out_shape, 2 * count * share, 2 * share)(
            in_specs=in_specs + [VMEM] * len(arrays), out_specs=out_specs, **more
        )(*operands, *arrays)

    total = jax.ShapeDtypeStruct((count, docs), jnp.float32)
    sums, hot, wide, docs_high = run(
        functools.partial(first_body, size=size),
        "scores_first",
        (
            total,
            jax.ShapeDtypeStruct((clusters, docs), jnp.bfloat16),
            total,
            pltpu.VMEM((docs - docs_low.shape[0], width), doc_grads.dtype),
        ),
        [own, (send(own[0], size, 1), [mask ^ 1 for mask in own[1]])],
        (me, docs_low, far_memory(doc_grads), topic_mask, membership.reshape(1, docs), owner_slot.reshape(1, clusters)),
        [SMEM, VMEM, HBM] + [VMEM] * 3,
        scratch_shapes=[pltpu.SemaphoreType.DMA((1,))],
    )
    both = (docs_low, near_memory(docs_high))
    arrays, masks = zip(*came)
    shape = (sum(a.shape[0] for a in arrays),) + arrays[0].shape[1:]
    held = call(stack_body, "stack", jax.ShapeDtypeStruct(shape, arrays[0].dtype), 0, 4 * math.prod(shape))(
        in_specs=[VMEM] * len(arrays) + [pl.BlockSpec(memory_space=pl.ANY)], out_specs=VMEM
    )(*arrays, sums)
    other = (send(held, size, 1), [mask ^ 1 for mask in sum(masks, [])])
    sums = run(next_body, "scores_next", total, came, (me, *both, sums), [SMEM] + [VMEM] * 3)
    shape = jax.ShapeDtypeStruct((size, clusters // size * count), jnp.float32)
    return run(last_body, "sums", shape, [other], (me, *both, sums, hot, wide), [SMEM] + [VMEM] * 5)


def per_device(doc_grads, val_grads, inv_hessian, topic_mask, membership, owner_slot, *, size):
    outer, inner = split(size)
    me = lax.axis_index("blk").astype(jnp.int32).reshape(1)
    docs = doc_grads.shape[0]
    val_local, width = val_grads.shape
    rows = inv_hessian.shape[0]
    clusters = owner_slot.shape[0]
    kept = clusters // size
    count = size * val_local
    half = rows // 2

    def both_body(val_ref, hess_ref, _, val_out, hess_out, sems):
        part = pl.ds(0, half)
        copies = [
            pltpu.make_async_copy(val_ref, val_out, sems.at[0]),
            pltpu.make_async_copy(hess_ref.at[part], hess_out.at[part], sems.at[1]),
        ]
        for copy in copies:
            copy.start()
        for copy in copies:
            copy.wait()

    shapes = tuple(pltpu.VMEM(x.shape, x.dtype) for x in (val_grads, inv_hessian))
    held, near_hess = call(both_body, "fetch", shapes, 0, 2 * rows * width, 1)(
        in_specs=[HBM, HBM, pl.BlockSpec(memory_space=pl.ANY)],
        out_specs=(VMEM, VMEM),
        scratch_shapes=[pltpu.SemaphoreType.DMA((2,))],
    )(far_memory(val_grads), far_memory(inv_hessian), me)
    held, near_hess = near_memory(held), near_memory(near_hess)
    order, outgoing = [0], val_grads
    stages = gather_stages(size)
    for k, stage in enumerate(stages):
        came = [send(outgoing, size, mask) for mask in stage]
        order += [mask ^ o for mask in stage for o in order]
        if k == 1:
            near_hess = fetch(inv_hessian, held, half, rows - half, into=near_hess)
        if stage is not stages[-1]:
            shape = ((len(came) + 1) * held.shape[0], width)
            held = call(pack_body, "pack", jax.ShapeDtypeStruct(shape, held.dtype), 0, 4 * shape[0] * width)(
                in_specs=[VMEM] * (len(came) + 1) + [pl.BlockSpec(memory_space=pl.ANY)], out_specs=VMEM
            )(held, *came, me if near_hess is None else near_hess)
            outgoing = held
    near = [held] + came
    early = docs // 2
    panel, docs_low = call(
        functools.partial(panel_body, order=order),
        "panel",
        (jax.ShapeDtypeStruct((count, rows), jnp.bfloat16), pltpu.VMEM((early, width), doc_grads.dtype)),
        2 * count * rows * width,
        2 * rows * width,
        16,
    )(
        in_specs=[SMEM] + [VMEM] * (len(near) + 1) + [HBM],
        out_specs=(VMEM, VMEM),
        scratch_shapes=[pltpu.SemaphoreType.DMA((1,))],
    )(me, *near, near_hess, far_memory(doc_grads))

    near, far, _ = stages
    own = jnp.stack([panel] + [send(panel, size, mask) for mask in near])
    own_masks = [0] + near
    came = [(send(own, size, mask), [mask ^ m for m in own_masks]) for mask in far]

    find = tiled_sums if rows % 128 == 0 else wide_sums
    given = (near_memory(docs_low), doc_grads) if rows % 128 == 0 else (doc_grads,)
    sums = find(me, (own, own_masks), came, *given, topic_mask, membership, owner_slot, size=size)

    sums = lax.all_to_all(sums.reshape(size, kept * count), "blk", 0, 0, tiled=True, axis_index_groups=[kept_by(size)])
    return call(total_body, "total", jax.ShapeDtypeStruct((kept, count), jnp.float32), 0, 8 * size * kept * count)(
        in_specs=[VMEM], out_specs=VMEM
    )(sums)


def solution(mesh):
    size = mesh.shape["blk"]

    def run(*args):
        return per_device(*args, size=size)

    in_specs = (
        P(("grp", "blk"), None),
        P("blk", None),
        P("blk", None),
        P(("grp", "blk"), None),
        P(("grp", "blk")),
        P(),
    )
    out_specs = P(("grp", "blk"), None)
    return jax.shard_map(run, mesh=mesh, in_specs=in_specs, out_specs=out_specs, check_vma=False)
```

```python
import functools
import math

import jax
import jax.numpy as jnp
from jax import lax
from jax.experimental import pallas as pl
from jax.experimental.pallas import tpu as pltpu
from jax.sharding import PartitionSpec as P

ROWS_BY_ROWS = (((1,), (1,)), ((), ()))
VMEM = pl.BlockSpec(memory_space=pltpu.VMEM)
HBM = pl.BlockSpec(memory_space=pltpu.HBM)
SMEM = pl.BlockSpec(memory_space=pltpu.SMEM)


def dot(a, b, dims=ROWS_BY_ROWS):
    return lax.dot_general(a, b, dims, preferred_element_type=jnp.float32)


def near_memory(x):
    return pltpu.with_memory_space_constraint(x, pltpu.VMEM)


def far_memory(x):
    return pltpu.with_memory_space_constraint(x, pltpu.HBM)


def call(body, name, out_shape, flops, moved, limit=12):
    return functools.partial(
        pl.pallas_call,
        body,
        out_shape=out_shape,
        compiler_params=pltpu.CompilerParams(vmem_limit_bytes=limit << 20),
        cost_estimate=pl.CostEstimate(flops=flops, bytes_accessed=moved, transcendentals=0),
        name=name,
    )


def send(x, size, mask):
    return lax.ppermute(x, "blk", [(i, i ^ mask) for i in range(size)])


def start_copies(ref, start, out, sems):
    pieces = sems.shape[0]
    rows = out.shape[0] // pieces
    copies = []
    for i in range(pieces):
        here, there = ref, out
        if ref.shape[0] != rows:
            here, there = ref.at[pl.ds(start + i * rows, rows)], out.at[pl.ds(i * rows, rows)]
        copies.append(pltpu.make_async_copy(here, there, sems.at[i]))
        copies[-1].start()
    return copies


def fetch(x, after, first=0, count=None, into=None):
    count = x.shape[0] - first if count is None else count

    def body(x_ref, *refs):
        out_ref, sems = refs[-2:]
        part = out_ref if count == out_ref.shape[0] else out_ref.at[pl.ds(first, count)]
        for copy in start_copies(x_ref, first, part, sems):
            copy.wait()

    run = call(body, "fetch", pltpu.VMEM(x.shape, x.dtype), 0, 2 * count * x.shape[1] * x.dtype.itemsize, 1)(
        in_specs=[HBM, pl.BlockSpec(memory_space=pl.ANY)] + [VMEM] * (into is not None),
        out_specs=VMEM,
        scratch_shapes=[pltpu.SemaphoreType.DMA((1,))],
        input_output_aliases={} if into is None else {2: 0},
    )
    return near_memory(run(far_memory(x), after, *([] if into is None else [into])))


def split(size):
    inner = 1
    while inner * inner * 4 <= size:
        inner *= 2
    return size // inner, inner


def stack_body(*refs):
    parts, out = refs[:-2], refs[-1]
    for i, part in enumerate(parts):
        n = part.shape[0]
        out[i * n : (i + 1) * n] = part[...]


def gather_stages(size):
    outer, inner = split(size)
    if inner < 2:
        return [[s * inner for s in range(1, outer)]]
    near = [2 * a + 1 for a in range(1, inner // 2)]
    far = [s * inner + 1 for s in range(1, outer)]
    if len(far) == 3:
        far = [far[0], far[2], far[1]]
    return [stage for stage in (near, far, [1]) if stage]


def pack_body(*refs):
    parts, out = refs[:-2], refs[-1]
    out[...] = jnp.concatenate([r[...].astype(jnp.float32) for r in parts], axis=0).astype(out.dtype)


def panel_body(me_ref, *refs, order):
    parts, hess_ref, docs_ref, out_ref, docs_out, sems = refs[:-5], *refs[-5:]
    copies = start_copies(docs_ref, 0, docs_out, sems)
    vals = jnp.concatenate([r[...].astype(jnp.float32) for r in parts], axis=0).astype(jnp.bfloat16)
    count = vals.shape[0]
    each = count // len(order)
    to = lax.broadcasted_iota(jnp.int32, (count, count), 0)
    at = lax.broadcasted_iota(jnp.int32, (count, count), 1)
    origin = jnp.zeros_like(at)
    for i, mask in enumerate(order):
        origin = jnp.where(at // each == i, mask, origin)
    place = (to == (me_ref[0] ^ origin) * each + at % each).astype(jnp.float32).astype(jnp.bfloat16)
    out_ref[...] = dot(place, dot(hess_ref[...], vals).astype(jnp.bfloat16)).astype(out_ref.dtype)
    for copy in copies:
        copy.wait()


def scores_of(me, docs_ref, parts):
    total = None
    for slices_ref, masks in parts:
        rows = slices_ref.shape[-1]
        for s, mask in enumerate(masks):
            column = pl.multiple_of((me ^ mask) * rows, rows)
            part = dot(slices_ref[s], docs_ref[:, pl.ds(column, rows)])
            total = part if total is None else total + part
    return total


def add_scores(me, docs_refs, parts):
    return jnp.concatenate([scores_of(me, r, parts) for r in docs_refs], axis=1)


def kept_by(size):
    outer, inner = split(size)
    groups = [*range(outer - 2, 0, -1), outer - 1, 0]
    return [g * inner + i for g in groups for i in range(inner - 1, -1, -1)]


def first_body(me_ref, low_ref, docs_ref, mask_ref, member_ref, slot_ref, *refs, masks, size):
    parts = list(zip(refs[: len(masks)], masks))
    out_ref, hot_ref, wide_ref, high_ref, sems = refs[len(masks) :]
    split_at = low_ref.shape[0]
    copies = start_copies(docs_ref, split_at, high_ref, sems)
    out_ref[:, :split_at] = scores_of(me_ref[0], low_ref, parts)
    clusters, docs = hot_ref.shape
    row = lax.broadcasted_iota(jnp.int32, (clusters, clusters), 0)
    kept = clusters // size
    owner = jnp.zeros_like(row)
    for i, device in enumerate(kept_by(size)):
        owner = jnp.where(row // kept == i, device, owner)
    slot = owner * kept + row % kept
    by_slot = (slot == slot_ref[...]).astype(jnp.float32).astype(jnp.bfloat16)
    cluster = lax.broadcasted_iota(jnp.int32, (clusters, docs), 0)
    by_doc = (cluster == member_ref[...]).astype(jnp.float32).astype(jnp.bfloat16)
    hot_ref[...] = dot(by_slot, by_doc, (((1,), (0,)), ((), ()))).astype(jnp.bfloat16)
    blocks = mask_ref.shape[0]
    doc = lax.broadcasted_iota(jnp.int32, (blocks, docs), 1)
    spread = (doc // (docs // blocks) == lax.broadcasted_iota(jnp.int32, (blocks, docs), 0)).astype(jnp.float32)
    narrow = mask_ref[...].astype(jnp.float32)
    wide_ref[...] = dot(narrow.astype(jnp.bfloat16), spread.astype(jnp.bfloat16), (((0,), (0,)), ((), ())))
    for copy in copies:
        copy.wait()
    out_ref[:, split_at:] = scores_of(me_ref[0], high_ref, parts)


def next_body(me_ref, low_ref, high_ref, sum_ref, *refs, masks):
    parts = list(zip(refs, masks))
    refs[-1][...] = sum_ref[...] + add_scores(me_ref[0], (low_ref, high_ref), parts)


def last_body(me_ref, low_ref, high_ref, sum_ref, hot_ref, wide_ref, *refs, masks):
    parts, out_ref = list(zip(refs, masks)), refs[-1]
    scores = sum_ref[...] + add_scores(me_ref[0], (low_ref, high_ref), parts)
    masked = 0.125 * (scores * wide_ref[...])
    high = masked.astype(jnp.bfloat16)
    low = (masked - high.astype(jnp.float32)).astype(jnp.bfloat16)
    out_ref[...] = dot(hot_ref[...], high) + dot(hot_ref[...], low)


def total_body(parts_ref, out_ref):
    kept, count = out_ref.shape
    total = jnp.sum(parts_ref[...], axis=0, keepdims=True)
    out_ref[...] = jnp.concatenate([total[:, r * count : (r + 1) * count] for r in range(kept)], axis=0)


def wide_sums(me, own, came, docs_in, topic_mask, membership, owner_slot, *, size):
    docs, width = docs_in.shape
    clusters = owner_slot.shape[0]
    arrays, masks = zip(own, *came)
    held, masks = jnp.concatenate(arrays), sum(masks, [])
    slices = jnp.concatenate([held, send(held, size, 1)])
    origins = me ^ jnp.array(masks + [mask ^ 1 for mask in masks])
    precond = jnp.moveaxis(slices[jnp.argsort(origins)], 0, 1).reshape(-1, width)
    blocks = topic_mask.shape[0]
    mask = jnp.repeat(topic_mask.T.astype(jnp.float32), docs // blocks, axis=1)
    mask = jnp.repeat(mask, precond.shape[0] // mask.shape[0], axis=0)
    masked = 0.125 * (dot(precond, docs_in) * mask)
    slot = jnp.arange(clusters).reshape(size, -1)[jnp.array(kept_by(size))].reshape(-1)
    by_slot = (slot[:, None] == owner_slot[None, :]).astype(jnp.bfloat16)
    by_doc = (jnp.arange(clusters)[:, None] == membership[None, :]).astype(jnp.bfloat16)
    hot = jnp.dot(by_slot, by_doc, preferred_element_type=jnp.float32).astype(jnp.bfloat16)
    return dot(hot, masked.astype(jnp.bfloat16))


def tiled_sums(me, own, came, docs_low, doc_grads, topic_mask, membership, owner_slot, *, size):
    docs, width = doc_grads.shape
    clusters = owner_slot.shape[0]
    count = own[0].shape[1]

    def run(body, name, out_shape, step, operands, in_specs, **more):
        arrays, masks = zip(*step)
        share = sum(len(m) for m in masks) * docs * width // size
        out_specs = (VMEM,) * len(out_shape) if isinstance(out_shape, tuple) else VMEM
        return call(functools.partial(body, masks=masks), name, out_shape, 2 * count * share, 2 * share)(
            in_specs=in_specs + [VMEM] * len(arrays), out_specs=out_specs, **more
        )(*operands, *arrays)

    total = jax.ShapeDtypeStruct((count, docs), jnp.float32)
    sums, hot, wide, docs_high = run(
        functools.partial(first_body, size=size),
        "scores_first",
        (
            total,
            jax.ShapeDtypeStruct((clusters, docs), jnp.bfloat16),
            total,
            pltpu.VMEM((docs - docs_low.shape[0], width), doc_grads.dtype),
        ),
        [own, (send(own[0], size, 1), [mask ^ 1 for mask in own[1]])],
        (me, docs_low, far_memory(doc_grads), topic_mask, membership.reshape(1, docs), owner_slot.reshape(1, clusters)),
        [SMEM, VMEM, HBM] + [VMEM] * 3,
        scratch_shapes=[pltpu.SemaphoreType.DMA((1,))],
    )
    both = (docs_low, near_memory(docs_high))
    arrays, masks = zip(*came)
    shape = (sum(a.shape[0] for a in arrays),) + arrays[0].shape[1:]
    held = call(stack_body, "stack", jax.ShapeDtypeStruct(shape, arrays[0].dtype), 0, 4 * math.prod(shape))(
        in_specs=[VMEM] * len(arrays) + [pl.BlockSpec(memory_space=pl.ANY)], out_specs=VMEM
    )(*arrays, sums)
    other = (send(held, size, 1), [mask ^ 1 for mask in sum(masks, [])])
    sums = run(next_body, "scores_next", total, came, (me, *both, sums), [SMEM] + [VMEM] * 3)
    shape = jax.ShapeDtypeStruct((clusters, count), jnp.float32)
    return run(last_body, "sums", shape, [other], (me, *both, sums, hot, wide), [SMEM] + [VMEM] * 5)


def per_device(doc_grads, val_grads, inv_hessian, topic_mask, membership, owner_slot, *, size):
    outer, inner = split(size)
    me = lax.axis_index("blk").astype(jnp.int32).reshape(1)
    docs = doc_grads.shape[0]
    val_local, width = val_grads.shape
    rows = inv_hessian.shape[0]
    clusters = owner_slot.shape[0]
    kept = clusters // size
    count = size * val_local
    half = rows * 3 // 8 // 16 * 16

    def both_body(val_ref, hess_ref, _, val_out, hess_out, sems):
        part = pl.ds(0, half)
        copies = [
            pltpu.make_async_copy(val_ref, val_out, sems.at[0]),
            pltpu.make_async_copy(hess_ref.at[part], hess_out.at[part], sems.at[1]),
        ]
        for copy in copies:
            copy.start()
        for copy in copies:
            copy.wait()

    shapes = tuple(pltpu.VMEM(x.shape, x.dtype) for x in (val_grads, inv_hessian))
    held, near_hess = call(both_body, "fetch", shapes, 0, 2 * rows * width, 1)(
        in_specs=[HBM, HBM, pl.BlockSpec(memory_space=pl.ANY)],
        out_specs=(VMEM, VMEM),
        scratch_shapes=[pltpu.SemaphoreType.DMA((2,))],
    )(far_memory(val_grads), far_memory(inv_hessian), me)
    held, near_hess = near_memory(held), near_memory(near_hess)
    order, outgoing = [0], val_grads
    stages = gather_stages(size)
    for k, stage in enumerate(stages):
        came = [send(outgoing, size, mask) for mask in stage]
        order += [mask ^ o for mask in stage for o in order]
        if k == 1:
            near_hess = fetch(inv_hessian, held, half, rows - half, into=near_hess)
        if stage is not stages[-1]:
            shape = ((len(came) + 1) * held.shape[0], width)
            held = call(pack_body, "pack", jax.ShapeDtypeStruct(shape, held.dtype), 0, 4 * shape[0] * width)(
                in_specs=[VMEM] * (len(came) + 1) + [pl.BlockSpec(memory_space=pl.ANY)], out_specs=VMEM
            )(held, *came, me if near_hess is None else near_hess)
            outgoing = held
    near = [held] + came
    early = docs * 5 // 8
    panel, docs_low = call(
        functools.partial(panel_body, order=order),
        "panel",
        (jax.ShapeDtypeStruct((count, rows), jnp.bfloat16), pltpu.VMEM((early, width), doc_grads.dtype)),
        2 * count * rows * width,
        2 * rows * width,
        16,
    )(
        in_specs=[SMEM] + [VMEM] * (len(near) + 1) + [HBM],
        out_specs=(VMEM, VMEM),
        scratch_shapes=[pltpu.SemaphoreType.DMA((1,))],
    )(me, *near, near_hess, far_memory(doc_grads))

    near, far, _ = stages
    own = jnp.stack([panel] + [send(panel, size, mask) for mask in near])
    own_masks = [0] + near
    came = [(send(own, size, mask), [mask ^ m for m in own_masks]) for mask in far]

    find = tiled_sums if rows % 128 == 0 else wide_sums
    given = (near_memory(docs_low), doc_grads) if rows % 128 == 0 else (doc_grads,)
    sums = find(me, (own, own_masks), came, *given, topic_mask, membership, owner_slot, size=size)

    sums = lax.all_to_all(sums.reshape(size, kept * count), "blk", 0, 0, tiled=True, axis_index_groups=[kept_by(size)])
    return call(total_body, "total", jax.ShapeDtypeStruct((kept, count), jnp.float32), 0, 8 * size * kept * count)(
        in_specs=[VMEM], out_specs=VMEM
    )(sums)


def solution(mesh):
    size = mesh.shape["blk"]

    def run(*args):
        return per_device(*args, size=size)

    in_specs = (
        P(("grp", "blk"), None),
        P("blk", None),
        P("blk", None),
        P(("grp", "blk"), None),
        P(("grp", "blk")),
        P(),
    )
    out_specs = P(("grp", "blk"), None)
    return jax.shard_map(run, mesh=mesh, in_specs=in_specs, out_specs=out_specs, check_vma=False)
```
